512 devices in a mesh: chol: 16 (over x_lo, z), row: 32 (over x_hi, y, core).
Axes of the slice: x: 4 (x_hi: 2, x_lo: 2; x = x_hi * 2 + x_lo), y: 8, z: 8, core: 2. Of those that a mesh axis runs over, the one named last changes fastest.
Arguments:
- chol_vectors: bfloat16 [16, 4096, 4096], P('chol', 'row'), may hold values from -0.796875 to 0.796875
- orbitals: bfloat16 [4096, 800], P('row'), may hold values from -1 to 1
- weights: float32 [800], replicated, may hold values from -1 to 1
Outputs:
- fock: float32 [4096, 4096], P('row', 'chol')
The draws below stay inside these ranges and needn't reach their ends.
All inputs are finite; a program needn't handle non-finite values.
Results may differ from the reference program's by a relative error of at most 0.0021.
Values may be sent and summed in bfloat16 or wider, within the bound.
A program may use at most 64 MiB of HBM per device.

```python
import jax
import jax.numpy as jnp
from jax import lax

NBF = 4096
NOCC = 800
NCHOL = 16


def draw_orbitals(key, part):
    key = jax.random.fold_in(key, 1)
    first = jax.random.fold_in(key, 0)
    position = jnp.arange(NBF, dtype=jnp.float32) / (NBF - 1)
    rising = (1.0 + 2.0 * position)[:, None]
    base = jax.random.normal(first, (NBF, NOCC), jnp.float32)
    return (base * rising * (0.5 * NBF ** (-0.5))).astype(jnp.bfloat16)


def spiked(drawn, own_key, source, target, blocks, factor):
    def block_of(dim):
        return (jnp.arange(drawn.shape[dim]) // (drawn.shape[dim] // blocks)).reshape((-1,) + (1,) * (drawn.ndim - 1 - dim))

    one_side = jax.random.permutation(own_key, blocks)[block_of(target)]
    second = (block_of(target) + blocks // 2) % blocks
    return jnp.where((block_of(source) == one_side) | (block_of(source) == second), factor * drawn, drawn)


def block_scale(key, shape, shards, least, high):
    factor_of, own = 1.0, jax.random.fold_in(key, 6)
    for dim, parts in shards:
        heights = jnp.exp(jax.random.uniform(jax.random.fold_in(own, dim), (parts,), jnp.float32, least / len(shards), high / len(shards)))
        factor_of = factor_of * jnp.repeat(heights, shape[dim] // parts).reshape([-1 if axis == dim else 1 for axis in range(len(shape))])
    return factor_of


def gaussian_with(own_key, shape, scale, reach, cuts, heavy, held_as=jnp.bfloat16):
    array = scale * jax.random.normal(own_key, shape, jnp.float32)
    if cuts:
        array = array * block_scale(own_key, shape, cuts, -0.22, 0.18)
    return jnp.clip(spiked(array, jax.random.fold_in(own_key, 3), *heavy), -reach, reach).astype(held_as)


def setup_inputs(seed: int = 0) -> dict:
    splits = jax.random.split(jax.random.key(seed), 4)
    return {
        "chol_vectors": gaussian_with(splits[0], (NCHOL, NBF, NBF), 0.137, 0.796875, ((0, 16), (1, 32)), (0, 2, 16, 2.0)),
        "orbitals": draw_orbitals(jax.random.fold_in(splits[3], 71), 0),
        "weights": jnp.clip(jax.random.uniform(splits[2], (NOCC,), jnp.float32, -1.0, 1.0), -1.0, 1.0),
    }


def reference(chol_vectors, orbitals, weights):
    orbital_f = orbitals.astype(jnp.float32)

    def add_vector(total, vector):
        half = jnp.dot(vector, orbitals, preferred_element_type=jnp.float32)
        gamma = jnp.sum(half * weights[None, :] * orbital_f)
        half_b = half.astype(jnp.bfloat16)
        scaled = (half * weights[None, :]).astype(jnp.bfloat16)
        exchange = jnp.dot(scaled, half_b.T, preferred_element_type=jnp.float32)
        return total + (2.0 * gamma * vector.astype(jnp.float32) - exchange), None

    start = jnp.zeros((NBF, NBF), jnp.float32)
    total, unused = lax.scan(add_vector, start, chol_vectors)
    return total
```

```python
import jax
import jax.numpy as jnp
from jax import lax
from jax.experimental import pallas as pl
from jax.experimental.pallas import tpu as pltpu
from jax.sharding import PartitionSpec as P

BF16, F32 = jnp.bfloat16, jnp.float32
OCC, HALF = 800, 400
FIRST = 208
PIECE = 48
CUT = 112
PARTS = ((0, FIRST), (FIRST, HALF - FIRST))
PLACE = {0: 0, 4: 1, 1: 2, 7: 3, 2: 4, 6: 5, 3: 6, 5: 7}
WAYS = (1, -1)
MESH = pl.DeviceIdType.MESH
NT = (((1,), (1,)), ((), ()))

names = {}
total = 0
for name, count in (
    ("ct_sib", 1), ("l_sib", 1), ("ct_x", 1), ("pieces", 8), ("pieces_x", 1),
    ("y", 2 * 2 * 5), ("z", 2 * 2 * 5), ("hx", 2), ("r", 2 * 8), ("ring", 2 * 2 * 5),
    ("sib", 2 * 8), ("g1", 8), ("g2", 8), ("lj", 8), ("rs", 16),
):
    names[name] = total
    total += count
SEMS = total


def kernel(l_ref, orb_ref, w_ref, out_ref, own, wcol, lbuf, ct, half, hb, hx, sc, sr, lhs, lj, g0, g1, g2, tiles, got, ss, rs, ls):
    c, r = lax.axis_index("chol"), lax.axis_index("row")
    l, z = c // 8, c % 8
    h, y, k = r // 16, (r // 2) % 8, r % 2

    def at(h=h, l=l, y=y, z=z, k=k):
        return (l * 8 + z, h * 16 + y * 2 + k)

    def copy(src, dst, sem, dev):
        return pltpu.make_async_remote_copy(
            src_ref=src, dst_ref=dst, send_sem=ss.at[sem], recv_sem=rs.at[sem], device_id=dev, device_id_type=MESH
        )

    started = []

    def send(src, dst, sem, dev):
        d = copy(src, dst, sem, dev)
        d.start()
        started.append(d)
        return d

    def wrap(v):
        return (v + 16) % 8

    flips = [(a, b, e) for a in (0, 1) for b in (0, 1) for e in (0, 1) if a + b + e]

    def flip(v, f):
        return 1 - v if f else v

    bar = pltpu.get_barrier_semaphore()

    def greet(dev):
        pl.semaphore_signal(bar, inc=1, device_id=dev, device_id_type=MESH)

    for a, b, e in flips:
        greet(at(h=flip(h, a), l=flip(l, b), k=flip(k, e)))
    for j in range(1, 8):
        greet(at(y=wrap(y + j)))
    for s in WAYS:
        greet(at(z=wrap(z + s)))
    mine = jnp.where(h == l, 1, 0)
    for j in range(8):
        greet(at(h=l, l=1 - l, z=wrap(z + j)))
    for j in range(1, 8):
        greet(at(h=l, l=l, z=wrap(z + j)))

    @pl.when(h != l)
    def _():
        greet(at(h=l, l=l))

    own[...] = jnp.transpose(orb_ref[...])
    wcol[...] = jnp.transpose(jnp.broadcast_to(w_ref[...], (128, OCC)))
    l_own = pltpu.make_async_copy(l_ref, lbuf.at[pl.ds(k * 128, 128)], ls.at[0])
    l_own.start()
    lanes_k = pl.ds(pl.multiple_of(k * 128, 128), 128)
    ct_own = pltpu.make_async_copy(own.at[pl.ds(k * HALF, HALF)], ct.at[0, :, lanes_k], ls.at[1])
    ct_own.start()
    pl.semaphore_wait(bar, 32 - mine)

    sib = at(k=1 - k)
    partner = at(h=1 - h, l=1 - l)
    ct_sib = send(own.at[pl.ds((1 - k) * HALF, HALF)], ct.at[0, :, lanes_k], names["ct_sib"], sib)
    l_sib = send(l_ref, lbuf.at[pl.ds(k * 128, 128)], names["l_sib"], sib)
    ct_own.wait()
    ct_sib.wait_recv()

    def y_rows(d, s):
        if d < 4:
            return pl.ds(0, FIRST)
        return pl.ds(0, CUT) if s == 1 else pl.ds(CUT, FIRST - CUT)

    def y_send(s, o, d):
        rows = y_rows(d + 1, s)
        src, dst = ct.at[o * 8 + (-s * d) % 8, rows], ct.at[o * 8 + (-s * (d + 1)) % 8, rows]
        send(src, dst, names["y"] + (0 if s == 1 else 10) + o * 5 + d + 1, at(y=wrap(y + s)))

    def y_wait(s, o, d):
        ref = ct.at[o * 8 + (-s * d) % 8, y_rows(d, s)]
        copy(ref, ref, names["y"] + (0 if s == 1 else 10) + o * 5 + d, at(y=wrap(y + s))).wait_recv()

    def z_ref(zz, first, count):
        rows = pl.ds(pl.multiple_of(FIRST + PIECE * (zz // 2), 16), PIECE)
        return ct.at[pl.ds(first, count), rows, pl.ds(pl.multiple_of((zz % 2) * 128, 128), 128)]

    def z_part(d, s, o):
        if d < 4:
            return (8, 8) if o else (1, 7)
        return (4 + 8 * o, 4) if s == 1 else (8 * o + (0 if o else 1), 4 if o else 3)

    def z_send(s, o, d):
        ref = z_ref(wrap(z - s * d), *z_part(d + 1, s, o))
        send(ref, ref, names["z"] + (0 if s == 1 else 10) + o * 5 + d + 1, at(z=wrap(z + s)))

    def z_wait(s, o, d):
        ref = z_ref(wrap(z - s * d), *z_part(d, s, o))
        copy(ref, ref, names["z"] + (0 if s == 1 else 10) + o * 5 + d, at(z=wrap(z + s))).wait_recv()

    piece = z_ref(z, 0, 1)
    pieces = [send(piece, z_ref(z, 8 - j, 1), names["pieces"] + j, at(y=wrap(y + j))) for j in range(1, 8)]
    ct_x = send(ct.at[0, pl.ds(0, FIRST)], ct.at[8, pl.ds(0, FIRST)], names["ct_x"], partner)
    for s in WAYS:
        y_send(s, 0, 0)
    for p in pieces:
        p.wait_recv()
    for s in WAYS:
        z_send(s, 0, 0)
    pieces_x = send(z_ref(z, 0, 8), z_ref(z, 8, 8), names["pieces_x"], partner)
    ct_x.wait_recv()
    for s in WAYS:
        y_send(s, 1, 0)
    pieces_x.wait_recv()
    for s in WAYS:
        z_send(s, 1, 0)

    lj_sems = []
    for n, (a, b, e) in enumerate(f for f in flips if f[2] == 0):
        hh, ll = flip(h, a), flip(l, b)
        for rel in range(8):
            start = pl.multiple_of(hh * 2048 + wrap(y + rel) * 256 + ll * 128, 128)
            d = copy(
                l_ref.at[:, pl.ds(start, 128)], lj.at[h * 2 + l, :, pl.ds(PLACE[rel] * 128, 128)],
                names["lj"] + 1 + a * 2 + b, at(h=hh, l=ll),
            )
            d.start()
        lj_sems.append((names["lj"] + 1 + a * 2 + b, hh, ll))
    for rel in range(8):
        start = pl.multiple_of(h * 2048 + wrap(y + rel) * 256 + l * 128, 128)
        pltpu.make_async_copy(
            l_ref.at[:, pl.ds(start, 128)], lj.at[h * 2 + l, :, pl.ds(PLACE[rel] * 128, 128)], ls.at[2]
        ).start()

    l_own.wait()
    l_sib.wait_recv()

    def product(b, lo, count):
        hh = jnp.where(b < 8, h, 1 - h)
        columns = pl.ds(pl.multiple_of((hh * 8 + (y + b) % 8) * 256, 256), 256)
        return lax.dot_general(ct[b, lo : lo + count], lbuf[:, columns], NT, preferred_element_type=F32)

    half[0:FIRST] = product(0, 0, FIRST) + product(8, 0, FIRST)

    for d in range(1, 5):
        for o in (0, 1):
            for s in WAYS:
                y_wait(s, o, d)
                if d < 4:
                    y_send(s, o, d)
            for s in WAYS:
                z_wait(s, o, d)
                if d < 4:
                    z_send(s, o, d)
            for s in WAYS if d < 4 else (1,):
                half[0:FIRST] += product(o * 8 + (-s * d) % 8, 0, FIRST)

    pieces_of_gamma = []

    def publish(u):
        lo, count = PARTS[u]
        here = half[lo : lo + count]
        w = wcol[pl.ds(pl.multiple_of(k * HALF + lo, 16), count)]
        weighted = here * jnp.concatenate([w, w], axis=1)
        rounded = here.astype(BF16)
        scaled = weighted.astype(BF16)
        pieces_of_gamma.append(jnp.sum(weighted * ct[0, lo : lo + count].astype(F32)))
        first, second = rounded[:, :128], rounded[:, 128:]
        rows = pl.ds(pl.multiple_of(k * HALF + lo, 16), count)
        hb[l, rows, 0:128] = jnp.where(l == 0, first, second)
        hx[lo : lo + count] = jnp.where(l == 0, second, first)
        sc[0, lo : lo + count] = scaled[:, :128]
        sc[1, lo : lo + count] = scaled[:, 128:]
        send(hx.at[pl.ds(lo, count)], hb.at[l, rows, pl.ds(0, 128)], names["hx"] + u, at(l=1 - l))
        for a, b, e in flips:
            send(
                sc.at[flip(k, e), pl.ds(lo, count)], sr.at[h * 2 + l, rows],
                names["r"] + u * 8 + a * 4 + b * 2 + e, at(h=flip(h, a), l=flip(l, b), k=flip(k, e)),
            )
        sr[h * 2 + l, rows] = jnp.where(k == 0, scaled[:, :128], scaled[:, 128:])

    def spot(u, rel, planes=None):
        lo, count = PARTS[u]
        rows = pl.ds(pl.multiple_of(k * HALF + lo, 16), count)
        lanes = pl.ds(PLACE[rel % 8] * 128, 128)
        return hb.at[:, rows, lanes] if planes is None else hb.at[pl.ds(planes, 1), rows, lanes]

    def ring_planes(d, s):
        return None if d < 4 else (0 if s == 1 else 1)

    def ring_sem(u, s, d):
        return names["ring"] + u * 10 + (0 if s == 1 else 5) + d

    def ring_send(u, s, d):
        planes = ring_planes(d + 1, s)
        send(spot(u, -s * d, planes), spot(u, -s * (d + 1), planes), ring_sem(u, s, d + 1), at(y=wrap(y + s)))

    def ring_wait(u, s, d):
        planes = ring_planes(d, s)
        ref = spot(u, -s * d, planes)
        copy(ref, ref, ring_sem(u, s, d), at(y=wrap(y + s))).wait_recv()

    def share(u, rel):
        send(spot(u, rel), spot(u, rel), names["sib"] + u * 8 + rel % 8, sib)

    def begin(u):
        lo, count = PARTS[u]
        rows = pl.ds(pl.multiple_of(k * HALF + lo, 16), count)
        copy(hx.at[pl.ds(lo, count)], hb.at[1 - l, rows, pl.ds(0, 128)], names["hx"] + u, at(l=1 - l)).wait_recv()
        for s in WAYS:
            ring_send(u, s, 0)
        share(u, 0)

    publish(0)

    half[FIRST:] = lax.fori_loop(
        0, 16, lambda b, acc: acc + product(b, FIRST, HALF - FIRST), jnp.zeros((HALF - FIRST, 256), F32)
    )
    begin(0)
    publish(1)
    g0[...] = jnp.broadcast_to(pieces_of_gamma[0] + pieces_of_gamma[1], (8, 128))
    g1[0] = g0[...]
    for j in range(1, 8):
        send(g0, g1.at[j], names["g1"] + j, at(y=wrap(y + j)))
    begin(1)
    for u in (0, 1):
        for s in WAYS:
            ring_wait(u, s, 1)
            ring_send(u, s, 1)
            share(u, -s)
    for j in range(1, 8):
        copy(g0, g1.at[j], names["g1"] + j, at(y=wrap(y + j))).wait_recv()
    me = l * 4 + h * 2 + k
    g2[me] = jnp.sum(g1[...], axis=0)
    for a, b, e in flips:
        send(g2.at[me], g2.at[me], names["g2"] + a * 4 + b * 2 + e, at(h=flip(h, a), l=flip(l, b), k=flip(k, e)))

    for u in (0, 1):
        lo, count = PARTS[u]
        for a, b, e in flips:
            ref = sr.at[0, pl.ds(lo, count)]
            copy(ref, ref, names["r"] + u * 8 + a * 4 + b * 2 + e, sib).wait_recv()
        if u == 0:
            for s in WAYS:
                ring_wait(0, s, 2)
                ring_send(0, s, 2)
                share(0, -s * 2)
    for hh in (0, 1):
        for ll in (0, 1):
            lhs[ll, hh * 128 : hh * 128 + 128] = jnp.transpose(sr[hh * 2 + ll])
    for s in WAYS:
        ring_wait(1, s, 2)
        ring_send(1, s, 2)
        share(1, -s * 2)

    for a, b, e in flips:
        copy(g2.at[0], g2.at[0], names["g2"] + a * 4 + b * 2 + e, sib).wait_recv()
    gamma = [2.0 * jnp.sum(g2[4 * ll : 4 * ll + 4], axis=0)[0:1] for ll in (0, 1)]
    for sem, hh, ll in lj_sems:
        copy(lj.at[0], lj.at[0], sem, sib).wait()
    pltpu.make_async_copy(lj.at[0], lj.at[0], ls.at[2]).wait()

    def tile_copy(place, hh, v):
        return pltpu.make_async_remote_copy(
            src_ref=tiles.at[place, hh], dst_ref=got.at[l * 8 + z],
            send_sem=ss.at[names["rs"] + place * 2 + hh], recv_sem=rs.at[names["rs"] + l * 8 + z],
            device_id=at(h=hh, l=h, z=v), device_id_type=MESH,
        )

    def fock(rels):
        for rel in rels:
            for u in (0, 1):
                ref = spot(u, rel)
                copy(ref, ref, names["sib"] + u * 8 + rel % 8, sib).wait_recv()
        lo = PLACE[rels[0]] * 128
        width = 128 * len(rels)
        terms = -jnp.dot(lhs[0], hb[0, :, lo : lo + width], preferred_element_type=F32)
        terms = terms - jnp.dot(lhs[1], hb[1, :, lo : lo + width], preferred_element_type=F32)
        for n, rel in enumerate(rels):
            place = PLACE[rel]
            v = wrap(y + rel)
            for hh in (0, 1):
                coulomb = sum(gamma[ll] * lj[hh * 2 + ll, :, place * 128 : place * 128 + 128].astype(F32) for ll in (0, 1))
                tile = terms[hh * 128 : hh * 128 + 128, n * 128 : n * 128 + 128] + coulomb
                tiles[place, hh] = tile.astype(BF16)
                same = (hh == h) & (l == h) & (v == z)
                out = tile_copy(place, hh, v)

                @pl.when(jnp.logical_not(same))
                def _():
                    out.start()

                @pl.when(same)
                def _():
                    got[l * 8 + z] = tiles[place, hh]

    fock((1, 7))
    for s in WAYS:
        ring_wait(0, s, 3)
        ring_send(0, s, 3)
        share(0, -s * 3)
    fock((2, 6))
    for s in WAYS:
        ring_wait(1, s, 3)
        ring_send(1, s, 3)
        share(1, -s * 3)
    fock((3, 5))
    for u in (0, 1):
        for s in WAYS:
            ring_wait(u, s, 4)
        share(u, 4)
    fock((0, 4))

    for ll in (0, 1):
        acc = None
        for j in range(8):
            zz = wrap(z + j)
            same = (h == l) & (ll == l) & (zz == z)

            @pl.when(jnp.logical_not(same))
            def _():
                pltpu.make_async_remote_copy(
                    src_ref=got.at[0], dst_ref=got.at[0], send_sem=ss.at[0], recv_sem=rs.at[names["rs"] + ll * 8 + zz],
                    device_id=sib, device_id_type=MESH,
                ).wait_recv()

            tile = got[ll * 8 + zz].astype(F32)
            acc = tile if acc is None else acc + tile
        out_ref[:, ll * 128 : ll * 128 + 128] = acc

    for d in started:
        d.wait_send()
    for rel in range(8):
        for hh in (0, 1):
            v = wrap(y + rel)

            @pl.when(jnp.logical_not((hh == h) & (l == h) & (v == z)))
            def _():
                tile_copy(PLACE[rel], hh, v).wait_send()


def on_device(chol_vectors, orbitals, weights):
    vmem = pl.BlockSpec(memory_space=pltpu.VMEM)
    return pl.pallas_call(
        kernel,
        out_shape=jax.ShapeDtypeStruct((128, 256), F32),
        in_specs=[pl.BlockSpec(memory_space=pl.ANY), vmem, vmem],
        out_specs=vmem,
        scratch_shapes=[
            pltpu.VMEM((OCC, 128), BF16),
            pltpu.VMEM((OCC, 128), F32),
            pltpu.VMEM((256, 4096), BF16),
            pltpu.VMEM((16, HALF, 256), BF16),
            pltpu.VMEM((HALF, 256), F32),
            pltpu.VMEM((2, OCC, 1024), BF16),
            pltpu.VMEM((HALF, 128), BF16),
            pltpu.VMEM((2, HALF, 128), BF16),
            pltpu.VMEM((4, OCC, 128), BF16),
            pltpu.VMEM((2, 256, OCC), BF16),
            pltpu.VMEM((4, 128, 1024), BF16),
            pltpu.VMEM((8, 128), F32),
            pltpu.VMEM((8, 8, 128), F32),
            pltpu.VMEM((8, 8, 128), F32),
            pltpu.VMEM((8, 2, 128, 128), BF16),
            pltpu.VMEM((16, 128, 128), BF16),
            pltpu.SemaphoreType.DMA((SEMS,)),
            pltpu.SemaphoreType.DMA((SEMS,)),
            pltpu.SemaphoreType.DMA((3,)),
        ],
        compiler_params=pltpu.CompilerParams(collective_id=0, has_side_effects=True, vmem_limit_bytes=48 << 20),
    )(chol_vectors.reshape(128, 4096), orbitals, weights.reshape(1, OCC))


def solution(mesh):
    return jax.shard_map(
        on_device,
        mesh=mesh,
        in_specs=(P("chol", "row", None), P("row", None), P()),
        out_specs=P("row", "chol"),
        check_vma=False,
    )
```
